32 devices in a mesh: section: 2 (over x), expert: 4 (over z), dp: 4 (over y, core).
Axes of the slice: x: 2, y: 2, z: 4, core: 2. Of those that a mesh axis runs over, the one named last changes fastest.
Arguments:
- ends: bfloat16 [2, 8192, 768], P('section', ('expert', 'dp')), may hold values from -6 to 6
- routes: int32 [2, 8192, 1], P('section', ('expert', 'dp')), may hold values from 0 to 7; in each aligned block of 256 rows (0 to 255, 256 to 511, ..., all dimensions but the last counted through in order) at most 64 rows name the same one
- norm_gain_first: bfloat16 [2, 768], P('section', 'dp'), may hold values from 0.5 to 1.5
- norm_gain_second: bfloat16 [2, 768], P('section', 'dp'), may hold values from 0.5 to 1.5
- w_query: bfloat16 [2, 768, 768], P('section', 'dp'), may hold values from -0.21875 to 0.21875
- w_key: bfloat16 [2, 768, 768], P('section', 'dp'), may hold values from -0.21875 to 0.21875
- w_value: bfloat16 [2, 768, 768], P('section', 'dp'), may hold values from -0.21875 to 0.21875
- w_output: bfloat16 [2, 768, 768], P('section', 'dp'), may hold values from -1.75 to 1.75
- w_router: bfloat16 [2, 768, 8], P('section', 'dp'), may hold values from -0.109375 to 0.109375
- bias_table: bfloat16 [2, 32, 12], P('section', 'dp'), may hold values from -4 to 4
- expert_in: bfloat16 [2, 8, 3072, 768], P('section', 'expert', 'dp'), may hold values from -0.21875 to 0.21875
- expert_out: bfloat16 [2, 8, 3072, 768], P('section', 'expert', 'dp'), may hold values from -4 to 4
Outputs:
- boundary: float32 [2, 8192, 768], P('section', ('expert', 'dp'))
- grad_gain_first: float32 [2, 768], P('section', 'dp')
- grad_gain_second: float32 [2, 768], P('section', 'dp')
- grad_query: float32 [2, 768, 768], P('section', 'dp')
- grad_key: float32 [2, 768, 768], P('section', 'dp')
- grad_value: float32 [2, 768, 768], P('section', 'dp')
- grad_output: float32 [2, 768, 768], P('section', 'dp')
- grad_router: float32 [2, 768, 8], P('section', 'dp')
- grad_table: float32 [2, 32, 12], P('section', 'dp')
- grad_expert_in: float32 [2, 8, 3072, 768], P('section', 'expert', 'dp')
- grad_expert_out: float32 [2, 8, 3072, 768], P('section', 'expert', 'dp')
The draws below stay inside these ranges and needn't reach their ends.
Inputs may be any that keep to these rules, and one draw needn't show every extreme that they name: `routes`: within each layer, among the 256 tokens of one sequence (aligned blocks of 256 rows) no expert is named more than 64 times, a bound that some block reaches.
All inputs are finite; a program needn't handle non-finite values.
Results may differ from the reference program's by a relative error of at most 0.03.
Values may be sent and summed in bfloat16 or wider, within the bound.
A program may use at most 256 MiB of HBM per device.

```python
import math
import jax
import jax.numpy as jnp
import numpy as np
from jax import lax

D = 768
HEADS = 12
FF = 3072
BUCKETS = 32
EXPERTS = 8
SEQ = 256
LAYERS = 2
CAP = 64
TOKENS = 8192


def shard_levels(key, extent, split, smallest, top_value):
    def one(axis_at, blocks):
        steps = jax.random.uniform(jax.random.fold_in(jax.random.fold_in(key, 6), axis_at), (blocks,), jnp.float32, smallest / len(split), top_value / len(split))
        return jnp.repeat(jnp.exp(steps), extent[axis_at] // blocks).reshape((-1,) + (1,) * (len(extent) - axis_at - 1))

    gain = one(*split[0])
    for cut in split[1:]:
        gain = gain * one(*cut)
    return gain


def routed_block(rng, own, number, rows, amount, top, bound, lean):
    sequence = jax.random.permutation(rng, amount)
    heavy_load, usual = portions_of(amount, rows * top, bound, lean, True), portions_of(amount, rows * top, bound, lean, False)
    places = jnp.arange(amount)

    def named(lengths, turn):
        used = int((lengths > 0).sum())
        fixed = max(1, used // 4)
        shifted = fixed + (places - fixed + turn * (used - fixed)) % max(1, amount - fixed)
        return jnp.zeros((amount,), jnp.int32).at[sequence[jnp.where(places < fixed, places, shifted)]].set(jnp.asarray(lengths, jnp.int32))

    lengths = jnp.where(number % 4 == 0, named(heavy_load, number // 4), named(usual, number - number // 4 - 1))
    mixed = jax.random.permutation(jax.random.fold_in(own, 3), amount)
    source_of, sink = mixed[0:amount // 2 * 2:2], mixed[1:amount // 2 * 2:2]
    slack = jnp.minimum(lengths[source_of] - 1, bound - lengths[sink]) // 2
    slack = jnp.where((source_of == sequence[0]) | (sink == sequence[0]) | (lengths[sink] == 0), 0, jnp.maximum(slack, 0))
    shifted = jax.random.randint(jax.random.fold_in(own, 4), (amount // 2,), 0, 1 << 20) % (slack + 1)
    lengths = lengths.at[source_of].add(-shifted).at[sink].add(shifted)
    items = jnp.searchsorted(jnp.cumsum(lengths), jnp.arange(rows * top), side="right").astype(jnp.int32)
    table = items.reshape(top, rows).T
    table = table[jax.random.permutation(jax.random.fold_in(own, 1), rows)]
    turn = jax.random.randint(jax.random.fold_in(own, 2), (rows, 1), 0, top)
    return jnp.take_along_axis(table, (jnp.arange(top)[None, :] + turn) % top, axis=1)


def portions_of(count, total, bound, lean, full):
    loads = [(1 << 20) // math.isqrt(grade ** lean) + 1 for grade in range(1, count + 1)]
    largest = bound if full else min(bound, max(-(-total // count), total * loads[0] // sum(loads)))
    least = 1 if total - largest >= count - 1 else 0
    given, rest = [largest] + [least] * (count - 1), total - largest - least * (count - 1)
    while rest > 0:
        candidates = [i for i in range(1, count) if given[i] < largest] or [i for i in range(1, count) if given[i] < bound]
        mass, budget = sum([loads[i] for i in candidates]), rest
        for i in candidates:
            addition = min(bound - given[i], max(1, budget * loads[i] // mass), rest)
            given[i] = given[i] + addition
            rest = rest - addition
    return np.array(given)


def scatter_about(rng, shape, deviation, bound, split=(), kind=jnp.bfloat16):
    factor_of = shard_levels(rng, shape, split, -0.22, 0.18) if split else 1.0
    entries = jax.random.normal(rng, shape, jnp.float32) * deviation * factor_of
    return jnp.minimum(jnp.maximum(entries, -bound), bound).astype(kind)


def setup_inputs(seed: int = 0) -> dict:
    seeds = jax.random.split(jax.random.key(seed), 13)
    ends = scatter_about(seeds[0], (2, TOKENS, D), 1.0, 6.0, ((0, 2), (1, 16)))
    routes_keys = jax.random.split(jax.random.fold_in(seeds[1], 1), LAYERS * TOKENS // SEQ)
    routes_turns = jax.random.permutation(jax.random.fold_in(seeds[1], 3), LAYERS * TOKENS // SEQ)
    routes = jax.vmap(lambda own, number: routed_block(jax.random.fold_in(seeds[1], 2), own, number, SEQ, EXPERTS, 1, CAP, 1))(routes_keys, routes_turns).reshape((LAYERS, TOKENS, 1))
    norm_gain_first = jnp.clip(1.0 + 0.1 * jax.random.normal(seeds[2], (LAYERS, D), jnp.float32), 0.5, 1.5).astype(jnp.bfloat16)
    norm_gain_second = jnp.clip(1.0 + 0.1 * jax.random.normal(seeds[3], (LAYERS, D), jnp.float32), 0.5, 1.5).astype(jnp.bfloat16)
    w_query = scatter_about(seeds[4], (LAYERS, D, D), D ** -0.5, 0.21875, ((0, 2), (1, 4)))
    w_key = scatter_about(seeds[5], (LAYERS, D, D), D ** -0.5, 0.21875, ((0, 2), (1, 4)))
    w_value = scatter_about(seeds[6], (LAYERS, D, D), D ** -0.5, 0.21875, ((0, 2), (1, 4)))
    w_output = scatter_about(seeds[7], (LAYERS, D, D), (D // 64) ** -0.5, 1.75, ((0, 2), (1, 4)))
    w_router = scatter_about(seeds[8], (LAYERS, D, EXPERTS), (4 * D) ** -0.5, 0.109375, ((0, 2), (1, 4)))
    bias_table = scatter_about(seeds[9], (LAYERS, BUCKETS, HEADS), 1.0, 4.0, ((0, 2), (1, 4)))
    expert_in = scatter_about(seeds[10], (LAYERS, EXPERTS, FF, D), D ** -0.5, 0.21875, ((0, 2), (1, 4), (2, 4)))
    expert_out = scatter_about(seeds[11], (LAYERS, EXPERTS, FF, D), (EXPERTS * 30 ** -1), 4.0, ((0, 2), (1, 4), (2, 4)))
    return dict(ends=ends, routes=routes, norm_gain_first=norm_gain_first, norm_gain_second=norm_gain_second, w_query=w_query, w_key=w_key, w_value=w_value, w_output=w_output, w_router=w_router, bias_table=bias_table, expert_in=expert_in, expert_out=expert_out)


@jax.custom_vjp
def low(v):
    return lax.optimization_barrier(v.astype(jnp.bfloat16)).astype(jnp.float32)

@jax.custom_vjp
def low_back(v):
    return v

def low_keep(v):
    return (low(v), None)

def low_pass(kept, grad):
    return (grad,)

def back_keep(v):
    return (v, None)

def back_low(kept, grad):
    return (low(grad),)
low.defvjp(low_keep, low_pass)
low_back.defvjp(back_keep, back_low)
EPSILON = 1e-06
PRECISE = lax.Precision.HIGHEST
LIMITS = (1, 2, 3, 4, 5, 6, 7, 8, 12, 16, 23, 32, 46, 64, 91)

def bucket_grid(length, buckets):
    positions = jnp.arange(length, dtype=jnp.int32)
    offsets = positions[:, None] - positions[None, :]
    distance = jnp.abs(offsets)
    bucket = jnp.where(offsets < 0, buckets // 2, 0).astype(jnp.int32)
    for threshold in LIMITS:
        bucket = bucket + (distance >= threshold).astype(jnp.int32)
    return bucket

def rms_norm(values, gain_value):
    return values * lax.rsqrt(lax.optimization_barrier(jnp.mean(values * values, axis=-1, keepdims=True)) + EPSILON) * gain_value

def attention(hidden, gain_value, w_query, w_key, w_value, w_output, position_bias):
    length, model_width = hidden.shape
    head_count = position_bias.shape[0]
    head_size = model_width // head_count
    factor = head_size ** (-0.5)
    normed = low(rms_norm(hidden, gain_value))

    def project(weight):
        return low_back(low(jnp.dot(normed, weight, precision=PRECISE))).reshape(length, head_count, head_size)
    queries = project(w_query)
    key_rows = project(w_key)
    value_rows = project(w_value)
    scores = jnp.einsum('qhd,khd->hqk', queries, key_rows, precision=PRECISE) * factor + position_bias
    shares = low(jax.nn.softmax(low_back(scores), axis=-1))
    attended = jnp.einsum('hqk,khd->qhd', shares, value_rows, precision=PRECISE).reshape(length, model_width)
    attended = low_back(low(attended))
    return hidden + low_back(jnp.dot(attended, w_output, precision=PRECISE))

def expert_block(operands):
    row_block, weight_in, weight_out = operands
    before = low_back(jnp.einsum('rd,fd->rf', row_block, weight_in, precision=PRECISE))
    activated = low(jax.nn.gelu(before))
    return jnp.dot(activated, weight_out, precision=PRECISE)

def layer(hidden, weights, targets):
    gain_first, gain_second, w_query, w_key, w_value, w_output, w_router, bias_rows, expert_in, expert_out = weights
    sequences, length, model_width = hidden.shape
    grid_values = bucket_grid(length, bias_rows.shape[0])
    position_bias = jnp.transpose(bias_rows[grid_values], (2, 0, 1))
    attend = jax.checkpoint(lambda member: attention(member, gain_first, w_query, w_key, w_value, w_output, position_bias))
    mixed = lax.map(attend, hidden)
    routed = low(rms_norm(mixed, gain_second))
    logits = low_back(jnp.einsum('nsd,de->nse', routed, w_router, precision=PRECISE))
    shares = jax.nn.softmax(logits, axis=-1)
    experts = w_router.shape[1]
    chosen = targets[:, :, None] == jnp.arange(experts, dtype=jnp.int32)[None, None, :]
    gate_value = lax.optimization_barrier(jnp.sum(jnp.where(chosen, shares, 0.0), axis=-1))
    counts = jnp.cumsum(chosen.astype(jnp.int32), axis=1).astype(jnp.int32)
    slot_rank = lax.optimization_barrier(jnp.sum(jnp.where(chosen, counts, 0), axis=-1)).astype(jnp.int32) - 1
    slot_index = (targets * CAP + slot_rank).astype(jnp.int32)

    def place(row_block, positions):
        return jnp.zeros((experts * CAP, model_width), jnp.float32).at[positions].set(row_block)
    buffers = low_back(jax.vmap(place)(routed, slot_index))
    grouped = jnp.transpose(buffers.reshape(sequences, experts, CAP, model_width), (1, 0, 2, 3))
    grouped = grouped.reshape(experts, sequences * CAP, model_width)
    produced = low_back(low(lax.map(jax.checkpoint(expert_block), (grouped, expert_in, expert_out))))
    returned = jnp.transpose(produced.reshape(experts, sequences, CAP, model_width), (1, 0, 2, 3))
    returned = returned.reshape(sequences, experts * CAP, model_width)
    fetched = jax.vmap(lambda row_block, positions: row_block[positions])(returned, slot_index)
    return mixed + gate_value[:, :, None] * fetched

def reference(ends, routes, norm_gain_first, norm_gain_second, w_query, w_key, w_value, w_output, w_router, bias_table, expert_in, expert_out):
    model_width = ends.shape[2]
    sequences = ends.shape[1] // SEQ
    weights = tuple((member.astype(jnp.float32) for member in (norm_gain_first, norm_gain_second, w_query, w_key, w_value, w_output, w_router, bias_table, expert_in, expert_out)))
    input_rows = ends[0].astype(jnp.float32).reshape(sequences, SEQ, model_width)
    cotangent = ends[1].astype(jnp.float32).reshape(sequences, SEQ, model_width)
    targets = routes[:, :, 0].reshape(routes.shape[0], sequences, SEQ)

    def forward(layer_input, params):
        middle = layer(layer_input, tuple((member[0] for member in params)), targets[0])
        middle = low_back(low(middle))
        return layer(middle, tuple((member[1] for member in params)), targets[1])
    result, pullback = jax.vjp(forward, input_rows, weights)
    grad_input, grad_weights = pullback(cotangent)
    boundary = jnp.stack([grad_input.reshape(-1, model_width), result.reshape(-1, model_width)])
    return (boundary, grad_weights[0], grad_weights[1], grad_weights[2], grad_weights[3], grad_weights[4], grad_weights[5], grad_weights[6], grad_weights[7], grad_weights[8], grad_weights[9])
```

```python
import jax
import jax.numpy as jnp
from jax import lax
from jax.experimental import pallas as pl
from jax.experimental.pallas import tpu as pltpu
from jax.sharding import PartitionSpec as P

SEQ = 256
MICRO = 2


EPSILON = 1e-06
LIMITS = (1, 2, 3, 4, 5, 6, 7, 8, 12, 16, 23, 32, 46, 64, 91)


def from_behind(block, axis, distance):
    devices = range(lax.axis_size(axis))
    route = [(i - distance, i) for i in devices if i - distance in devices]
    return lax.ppermute(block, axis, route)


def bucket_grid(length, buckets):
    positions = jnp.arange(length, dtype=jnp.int32)
    offsets = positions[:, None] - positions[None, :]
    distance = jnp.abs(offsets)
    bucket = jnp.where(offsets < 0, buckets // 2, 0).astype(jnp.int32)
    for threshold in LIMITS:
        bucket = bucket + (distance >= threshold).astype(jnp.int32)
    return bucket


def bias_of(bias_rows, length):
    buckets = bias_rows.shape[0]
    grid_values = bucket_grid(length, buckets)[None]
    bias = jnp.broadcast_to(bias_rows[0][:, None, None], (bias_rows.shape[1], length, length))
    for number in range(1, buckets):
        bias = jnp.where(grid_values == number, bias_rows[number][:, None, None], bias)
    return bias


def bucket_sums(grid_grads, buckets):
    head_count, length, _ = grid_grads.shape

    def kernel(grads_ref, table_ref):
        grid_values = bucket_grid_iota(length, buckets)
        grads = grads_ref[0]
        rows = [
            jnp.sum(jnp.where(grid_values == number, grads, 0.0), axis=0, keepdims=True)
            for number in range(buckets)
        ]
        table_ref[0] = jnp.concatenate(rows, axis=0)

    partial = pl.pallas_call(
        kernel,
        grid=(head_count,),
        out_shape=jax.ShapeDtypeStruct((head_count, buckets, length), jnp.float32),
        in_specs=[pl.BlockSpec((1, length, length), lambda h: (h, 0, 0))],
        out_specs=pl.BlockSpec((1, buckets, length), lambda h: (h, 0, 0)),
        compiler_params=pltpu.CompilerParams(vmem_limit_bytes=16 * 1024 * 1024),
        cost_estimate=pl.CostEstimate(
            flops=3 * buckets * grid_grads.size, bytes_accessed=5 * grid_grads.size, transcendentals=0
        ),
    )(grid_grads)
    return jnp.sum(partial, axis=-1).T


def bucket_grid_iota(length, buckets):
    offsets = lax.broadcasted_iota(jnp.int32, (length, length), 0) - lax.broadcasted_iota(
        jnp.int32, (length, length), 1
    )
    distance = jnp.abs(offsets)
    bucket = jnp.where(offsets < 0, buckets // 2, 0).astype(jnp.int32)
    for threshold in LIMITS:
        bucket = bucket + (distance >= threshold).astype(jnp.int32)
    return bucket


def root_scale(values):
    return lax.rsqrt(jnp.mean(values * values, axis=-1, keepdims=True) + EPSILON)


def norm_backward(grad_normed, values, factor, gain_value):
    scaled = grad_normed * gain_value
    grad_gain = jnp.sum(grad_normed * values * factor, axis=0)
    grad_values = factor * scaled - values * factor * factor * factor * jnp.mean(
        scaled * values, axis=-1, keepdims=True
    )
    return (grad_values, grad_gain)


def to_owners(outgoing, local_experts):
    experts_rows, model_width = outgoing.shape
    owners = lax.axis_size("expert")
    capacity = experts_rows // (owners * local_experts)
    received = lax.all_to_all(
        outgoing.reshape(owners, local_experts, capacity, model_width),
        "expert",
        split_axis=0,
        concat_axis=0,
        tiled=True,
    )
    return received.transpose(1, 0, 2, 3).reshape(local_experts, owners * capacity, model_width)


def to_tokens(produced):
    local_experts, rows, model_width = produced.shape
    owners = lax.axis_size("expert")
    capacity = rows // owners
    returned = lax.all_to_all(
        produced.reshape(local_experts, owners, capacity, model_width).transpose(1, 0, 2, 3),
        "expert",
        split_axis=0,
        concat_axis=0,
        tiled=True,
    )
    return returned.reshape(owners * local_experts * capacity, model_width)


def expert_forward(grouped, w_in_use, w_out_use):
    before = jnp.einsum("erd,efd->erf", grouped, w_in_use, preferred_element_type=jnp.float32)
    activated = jax.nn.gelu(before).astype(jnp.bfloat16)
    produced = jnp.einsum("erf,efd->erd", activated, w_out_use, preferred_element_type=jnp.float32)
    return (produced.astype(jnp.bfloat16), (grouped, before, activated))


def expert_backward(grad_rows, before, w_in_use, w_out_use):
    grad_activated = jnp.einsum(
        "erd,efd->erf", grad_rows, w_out_use, preferred_element_type=jnp.float32
    )
    grad_before = jax.vjp(jax.nn.gelu, before)[1](grad_activated)[0].astype(jnp.bfloat16)
    grad_inputs = jnp.einsum(
        "erf,efd->erd", grad_before, w_in_use, preferred_element_type=jnp.float32
    )
    return (grad_inputs.astype(jnp.bfloat16), grad_before)


def dispatch_of(targets, experts):
    length = targets.shape[0]
    capacity = max(2, 2 * length // experts)
    chosen = targets[:, None] == jnp.arange(experts, dtype=jnp.int32)[None, :]
    positions = jnp.arange(length, dtype=jnp.int32)
    earlier = (positions[:, None] > positions[None, :]).astype(jnp.bfloat16)
    counts = jnp.dot(earlier, chosen.astype(jnp.bfloat16), preferred_element_type=jnp.float32)
    slot_rank = jnp.sum(jnp.where(chosen, counts, 0.0), axis=-1).astype(jnp.int32)
    slot_index = targets * capacity + slot_rank
    slots = jnp.arange(experts * capacity, dtype=jnp.int32)
    placement = (slots[:, None] == slot_index[None, :]).astype(jnp.bfloat16)
    return (chosen, placement)


def place(placement, rows):
    return jnp.dot(placement, rows, preferred_element_type=jnp.float32).astype(jnp.bfloat16)


def fetch(placement, rows):
    return jnp.einsum("bs,bd->sd", placement, rows, preferred_element_type=jnp.float32)


def layer_forward(arriving, dispatch, mixer_set, position_bias, w_in_use, w_out_use):
    gain_first, gain_second, w_project, w_output, w_router = mixer_set
    hidden = arriving.astype(jnp.float32)
    length, model_width = hidden.shape
    head_count = position_bias.shape[0]
    head_size = model_width // head_count
    head_shape = (length, head_count, head_size)
    factor = head_size ** (-0.5)
    first_scale = root_scale(hidden)
    normed = (hidden * first_scale * gain_first.astype(jnp.float32)).astype(jnp.bfloat16)
    projected = jnp.dot(normed, w_project, preferred_element_type=jnp.float32).astype(jnp.bfloat16)
    queries, key_rows, value_rows = jnp.split(projected, 3, axis=1)
    scores = (
        jnp.einsum(
            "qhd,khd->hqk",
            queries.reshape(head_shape),
            key_rows.reshape(head_shape),
            preferred_element_type=jnp.float32,
        )
        * factor
        + position_bias
    )
    row_peak = jnp.max(scores, axis=-1, keepdims=True)
    log_total = row_peak + jnp.log(jnp.sum(jnp.exp(scores - row_peak), axis=-1, keepdims=True))
    shares = jnp.exp(scores - log_total).astype(jnp.bfloat16)
    attended = jnp.einsum(
        "hqk,khd->qhd", shares, value_rows.reshape(head_shape), preferred_element_type=jnp.float32
    )
    attended = attended.reshape(length, model_width).astype(jnp.bfloat16)
    mixed = hidden + jnp.dot(attended, w_output, preferred_element_type=jnp.float32)
    second_scale = root_scale(mixed)
    routed = (mixed * second_scale * gain_second.astype(jnp.float32)).astype(jnp.bfloat16)
    logits = jnp.dot(routed, w_router, preferred_element_type=jnp.float32)
    router = jax.nn.softmax(logits, axis=-1)
    chosen, placement = dispatch
    gate_value = jnp.sum(jnp.where(chosen, router, 0.0), axis=-1)
    grouped = to_owners(place(placement, routed), w_in_use.shape[0])
    produced, kept_rows = expert_forward(grouped, w_in_use, w_out_use)
    fetched = fetch(placement, to_tokens(produced))
    result = mixed + gate_value[:, None] * fetched
    stored = (
        hidden,
        normed,
        first_scale,
        queries,
        key_rows,
        value_rows,
        log_total,
        attended,
        mixed,
        second_scale,
        routed,
        router,
        chosen,
        gate_value,
        placement,
        fetched,
        kept_rows,
    )
    return (result, stored)


def layer_backward(grad_out, stored, mixer_set, position_bias, w_in_use, w_out_use):
    gain_first, gain_second, w_project, w_output, w_router = mixer_set
    (
        hidden,
        normed,
        first_scale,
        queries,
        key_rows,
        value_rows,
        log_total,
        attended,
        mixed,
        second_scale,
        routed,
        router,
        chosen,
        gate_value,
        placement,
        fetched,
        kept_rows,
    ) = stored
    length, model_width = hidden.shape
    head_count = position_bias.shape[0]
    head_size = model_width // head_count
    head_shape = (length, head_count, head_size)
    factor = head_size ** (-0.5)
    grad_gate = jnp.sum(grad_out * fetched, axis=-1)
    grad_fetched = (gate_value[:, None] * grad_out).astype(jnp.bfloat16)
    grouped, before, activated = kept_rows
    grad_rows = to_owners(place(placement, grad_fetched), w_in_use.shape[0])
    grad_inputs, grad_before = expert_backward(grad_rows, before, w_in_use, w_out_use)
    grad_routed = fetch(placement, to_tokens(grad_inputs))
    grad_logits = (
        (gate_value * grad_gate)[:, None] * (chosen.astype(jnp.float32) - router)
    ).astype(jnp.bfloat16)
    grad_routed = grad_routed + jnp.einsum(
        "se,de->sd", grad_logits, w_router, preferred_element_type=jnp.float32
    )
    norm_grad, grad_gain_second = norm_backward(
        grad_routed, mixed, second_scale, gain_second.astype(jnp.float32)
    )
    grad_mixed = grad_out + norm_grad
    grad_branch = grad_mixed.astype(jnp.bfloat16)
    grad_attended = jnp.einsum(
        "se,de->sd", grad_branch, w_output, preferred_element_type=jnp.float32
    )
    grad_attended = grad_attended.astype(jnp.bfloat16).reshape(head_shape)
    query_heads = queries.reshape(head_shape)
    key_heads = key_rows.reshape(head_shape)
    scores = (
        jnp.einsum("qhd,khd->hqk", query_heads, key_heads, preferred_element_type=jnp.float32)
        * factor
        + position_bias
    )
    softmax_rows = jnp.exp(scores - log_total)
    shares = softmax_rows.astype(jnp.bfloat16)
    grad_values = jnp.einsum(
        "hqk,qhd->khd", shares, grad_attended, preferred_element_type=jnp.float32
    )
    grad_values = grad_values.astype(jnp.bfloat16).reshape(length, model_width)
    grad_shares = jnp.einsum(
        "qhd,khd->hqk",
        grad_attended,
        value_rows.reshape(head_shape),
        preferred_element_type=jnp.float32,
    )
    grad_scores = softmax_rows * (
        grad_shares - jnp.sum(grad_shares * softmax_rows, axis=-1, keepdims=True)
    )
    grad_scores = grad_scores.astype(jnp.bfloat16)
    grad_queries = (
        jnp.einsum("hqk,khd->qhd", grad_scores, key_heads, preferred_element_type=jnp.float32)
        * factor
    )
    grad_queries = grad_queries.astype(jnp.bfloat16).reshape(length, model_width)
    grad_keys = (
        jnp.einsum("hqk,qhd->khd", grad_scores, query_heads, preferred_element_type=jnp.float32)
        * factor
    )
    grad_keys = grad_keys.astype(jnp.bfloat16).reshape(length, model_width)
    grad_projected = jnp.concatenate([grad_queries, grad_keys, grad_values], axis=1)
    grad_normed = jnp.einsum(
        "se,de->sd", grad_projected, w_project, preferred_element_type=jnp.float32
    )
    first_grad, grad_gain_first = norm_backward(
        grad_normed, hidden, first_scale, gain_first.astype(jnp.float32)
    )
    grad_hidden = grad_mixed + first_grad
    kept = dict(
        gains=jnp.stack([grad_gain_first, grad_gain_second], axis=1),
        grad_scores=grad_scores,
        normed=normed,
        grad_projected=grad_projected,
        attended=attended,
        grad_branch=grad_branch,
        routed=routed,
        grad_logits=grad_logits,
    )
    return (grad_hidden, kept, dict(
        grouped=grouped, activated=activated, grad_rows=grad_rows, grad_before=grad_before
    ))


def scatter_sum(full, axis):
    return lax.psum_scatter(full, "dp", scatter_dimension=axis, tiled=True)


def weight_grad(operands, grads):
    return jnp.einsum("sd,se->de", operands, grads, preferred_element_type=jnp.float32)


def reduce_mixer(rows, sums, buckets):
    project = weight_grad(rows["normed"], rows["grad_projected"])
    output = weight_grad(rows["attended"], rows["grad_branch"])
    router = weight_grad(rows["routed"], rows["grad_logits"])
    table = bucket_sums(sums["grad_scores"], buckets)
    small = pack_small([router, sums["gains"]], table)
    packed = jnp.concatenate([project, output, small], axis=1).astype(jnp.bfloat16)
    total = lax.psum(scatter_sum(packed, 0), "expert").astype(jnp.float32)
    width = total.shape[0] * lax.axis_size("dp")
    query, key, value, output = (total[:, i * width : (i + 1) * width] for i in range(4))
    router, gains, table = unpack_small(
        total[:, 4 * width :], [router.shape[1], 2], table.shape, 1
    )
    return (gains[:, 0], gains[:, 1], query, key, value, output, router, table)


def pack_small(columns, table, shards=None):
    rows = columns[0].shape[0]
    shards = lax.axis_size("dp") if shards is None else shards
    own = table.reshape(shards, table.shape[0] // shards, table.shape[1])
    own = jnp.pad(own, ((0, 0), (0, rows // shards - own.shape[1]), (0, 0)))
    packed = jnp.concatenate([*columns, own.reshape(rows, table.shape[1])], axis=1)
    return jnp.pad(packed, ((0, 0), (0, -packed.shape[1] % 128)))


def unpack_small(packed, widths, table_shape, shards):
    found = []
    start = 0
    for width in widths:
        found.append(packed[:, start : start + width])
        start += width
    table_rows, heads = table_shape
    table_rows = table_rows * shards // lax.axis_size("dp")
    table = packed[:, start : start + heads].reshape(shards, -1, heads)
    found.append(table[:, : table_rows // shards].reshape(table_rows, heads))
    return found


def local(
    ends,
    routes,
    norm_gain_first,
    norm_gain_second,
    w_query,
    w_key,
    w_value,
    w_output,
    w_router,
    bias_table,
    expert_in,
    expert_out,
):
    is_first = lax.axis_index("section") == 0
    model_width = ends.shape[2]
    shards = lax.axis_size("dp")
    experts = w_router.shape[2]
    gains = jnp.stack([norm_gain_first[0], norm_gain_second[0]], axis=1)
    small = pack_small([w_router[0], gains], bias_table[0], 1)
    packed = jnp.concatenate([w_query[0], w_key[0], w_value[0], w_output[0], small], axis=1)
    packed = lax.all_gather(packed, "dp", axis=0, tiled=True)
    w_in_use = lax.all_gather(expert_in[0], "dp", axis=1, tiled=True)
    w_out_use = lax.all_gather(expert_out[0], "dp", axis=1, tiled=True)
    buckets = bias_table.shape[1] * shards
    router_full, gains, bias_rows = unpack_small(
        packed[:, 4 * model_width :],
        [experts, 2],
        (buckets * shards // shards, bias_table.shape[2]),
        shards,
    )
    mixer_set = (
        gains[:, 0],
        gains[:, 1],
        packed[:, : 3 * model_width],
        packed[:, 3 * model_width : 4 * model_width],
        router_full,
    )
    position_bias = bias_of(bias_rows.astype(jnp.float32), SEQ)
    local_rows = ends[0]
    local_routes = routes[0, :, 0]

    def block_rows(source, micro_index):
        return source[micro_index * SEQ : (micro_index + 1) * SEQ]

    dispatches = [dispatch_of(block_rows(local_routes, m), experts) for m in range(MICRO)]
    stored_list = []
    results = []
    arriving = jnp.zeros((SEQ, model_width), jnp.bfloat16)
    for tick_number in range(MICRO + 1):
        own_micro = min(tick_number, MICRO - 1)
        prior_micro = max(tick_number - 1, 0)
        layer_input = jnp.where(is_first, block_rows(local_rows, own_micro), arriving)
        dispatch = jax.tree.map(
            lambda own, prior: jnp.where(is_first, own, prior),
            dispatches[own_micro],
            dispatches[prior_micro],
        )
        result, stored = layer_forward(
            layer_input, dispatch, mixer_set, position_bias, w_in_use, w_out_use
        )
        stored_list.append(stored)
        results.append(result)
        if tick_number < MICRO:
            arriving = from_behind(result.astype(jnp.bfloat16), "section", 1)
    input_grads = [None] * MICRO
    returning = jnp.zeros((SEQ, model_width), jnp.bfloat16)
    mixer_kept = []
    expert_kept = []
    for step_number in range(MICRO + 1):
        if step_number < MICRO:
            cotangent = block_rows(local_rows, MICRO - 1 - step_number).astype(jnp.float32)
        else:
            cotangent = jnp.zeros((SEQ, model_width), jnp.float32)
        grad_out = jnp.where(is_first, returning.astype(jnp.float32), cotangent)
        grad_hidden, kept_mixer, kept_expert = layer_backward(
            grad_out,
            stored_list[MICRO - step_number],
            mixer_set,
            position_bias,
            w_in_use,
            w_out_use,
        )
        if step_number < MICRO:
            returning = from_behind(grad_hidden.astype(jnp.bfloat16), "section", -1)
        if step_number >= 1:
            input_grads[MICRO - step_number] = grad_hidden
        mixer_kept.append(kept_mixer)
        expert_kept.append(kept_expert)

    def real(kept, name):
        return (kept[1][name], jnp.where(is_first, kept[2][name], kept[0][name]))

    experts_rows = {
        name: jnp.concatenate(real(expert_kept, name), axis=1) for name in expert_kept[0]
    }
    grad_out_full = jnp.einsum(
        "erf,erd->efd",
        experts_rows["activated"],
        experts_rows["grad_rows"],
        preferred_element_type=jnp.float32,
    )
    grad_w_out = scatter_sum(grad_out_full.astype(jnp.bfloat16), 1).astype(jnp.float32)
    grad_in_full = jnp.einsum(
        "erf,erd->efd",
        experts_rows["grad_before"],
        experts_rows["grouped"],
        preferred_element_type=jnp.float32,
    )
    grad_w_in = scatter_sum(grad_in_full.astype(jnp.bfloat16), 1).astype(jnp.float32)
    expert_sum = (grad_w_in, grad_w_out)
    summed = ("gains", "grad_scores")
    sums = {
        name: sum(part.astype(jnp.float32) for part in real(mixer_kept, name)) for name in summed
    }
    rows = {
        name: jnp.concatenate(real(mixer_kept, name), axis=0)
        for name in mixer_kept[0]
        if name not in summed
    }
    mixer_sum = reduce_mixer(rows, sums, buckets)
    pieces = [
        jnp.where(is_first, input_grads[micro_index], results[micro_index + 1])
        for micro_index in range(MICRO)
    ]
    boundary = jnp.concatenate(pieces, axis=0)[None]
    return (
        boundary,
        mixer_sum[0][None],
        mixer_sum[1][None],
        mixer_sum[2][None],
        mixer_sum[3][None],
        mixer_sum[4][None],
        mixer_sum[5][None],
        mixer_sum[6][None],
        mixer_sum[7][None],
        expert_sum[0][None],
        expert_sum[1][None],
    )


def solution(mesh):
    in_specs = (
        P("section", ("expert", "dp"), None),
        P("section", ("expert", "dp"), None),
        P("section", "dp"),
        P("section", "dp"),
        P("section", "dp", None),
        P("section", "dp", None),
        P("section", "dp", None),
        P("section", "dp", None),
        P("section", "dp", None),
        P("section", "dp", None),
        P("section", "expert", "dp", None),
        P("section", "expert", "dp", None),
    )
    out_specs = (
        P("section", ("expert", "dp"), None),
        P("section", "dp"),
        P("section", "dp"),
        P("section", "dp", None),
        P("section", "dp", None),
        P("section", "dp", None),
        P("section", "dp", None),
        P("section", "dp", None),
        P("section", "dp", None),
        P("section", "expert", "dp", None),
        P("section", "expert", "dp", None),
    )
    return jax.shard_map(local, mesh=mesh, in_specs=in_specs, out_specs=out_specs, check_vma=False)
```

```python
import jax
import jax.numpy as jnp
import numpy as np
from jax import lax
from jax.experimental import pallas as pl
from jax.experimental.pallas import tpu as pltpu
from jax.sharding import PartitionSpec as P

SEQ = 256
MICRO = 2


EPSILON = 1e-06
LIMITS = (1, 2, 3, 4, 5, 6, 7, 8, 12, 16, 23, 32, 46, 64, 91)


def from_behind(block, axis, distance):
    devices = range(lax.axis_size(axis))
    route = [(i - distance, i) for i in devices if i - distance in devices]
    return lax.ppermute(block, axis, route)


def bucket_grid(length, buckets):
    positions = jnp.arange(length, dtype=jnp.int32)
    offsets = positions[:, None] - positions[None, :]
    distance = jnp.abs(offsets)
    bucket = jnp.where(offsets < 0, buckets // 2, 0).astype(jnp.int32)
    for threshold in LIMITS:
        bucket = bucket + (distance >= threshold).astype(jnp.int32)
    return bucket


def bias_of(bias_rows, length):
    buckets = bias_rows.shape[0]
    grid_values = bucket_grid(length, buckets)[None]
    bias = jnp.broadcast_to(bias_rows[0][:, None, None], (bias_rows.shape[1], length, length))
    for number in range(1, buckets):
        bias = jnp.where(grid_values == number, bias_rows[number][:, None, None], bias)
    return bias


def bucket_sums(grid_grads, buckets):
    head_count, length, _ = grid_grads.shape
    high, wide = 8, 128
    positions = np.arange(length)
    offsets = positions[:, None] - positions[None, :]
    known = np.where(offsets < 0, buckets // 2, 0)
    for threshold in LIMITS:
        known = known + (np.abs(offsets) >= threshold)

    def kernel(grid_ref, grads_ref, table_ref):
        sums = [None] * buckets
        for top in range(0, length, high):
            for left in range(0, length, wide):
                block = (slice(top, top + high), slice(left, left + wide))
                present = np.unique(known[block])
                grads = grads_ref[(0,) + block]
                named = grid_ref[block] if len(present) > 1 else None
                for number in present.tolist():
                    own = grads if named is None else jnp.where(named == number, grads, 0.0)
                    sums[number] = own if sums[number] is None else sums[number] + own
        empty = jnp.zeros((1, wide), jnp.float32)
        table_ref[0] = jnp.concatenate(
            [empty if own is None else jnp.sum(own, axis=0, keepdims=True) for own in sums], axis=0
        )

    partial = pl.pallas_call(
        kernel,
        grid=(head_count,),
        out_shape=jax.ShapeDtypeStruct((head_count, buckets, wide), jnp.float32),
        in_specs=[
            pl.BlockSpec((length, length), lambda h: (0, 0)),
            pl.BlockSpec((1, length, length), lambda h: (h, 0, 0)),
        ],
        out_specs=pl.BlockSpec((1, buckets, wide), lambda h: (h, 0, 0)),
        compiler_params=pltpu.CompilerParams(vmem_limit_bytes=16 * 1024 * 1024),
        cost_estimate=pl.CostEstimate(
            flops=30 * grid_grads.size, bytes_accessed=5 * grid_grads.size, transcendentals=0
        ),
    )(bucket_grid(length, buckets), grid_grads)
    return jnp.sum(partial, axis=-1).T


def root_scale(values):
    return lax.rsqrt(jnp.mean(values * values, axis=-1, keepdims=True) + EPSILON)


def norm_backward(grad_normed, values, factor, gain_value):
    scaled = grad_normed * gain_value
    grad_gain = jnp.sum(grad_normed * values * factor, axis=0)
    grad_values = factor * scaled - values * factor * factor * factor * jnp.mean(
        scaled * values, axis=-1, keepdims=True
    )
    return (grad_values, grad_gain)


def from_partner(block, bit):
    return lax.ppermute(block, "dp", [(i, i ^ bit) for i in range(lax.axis_size("dp"))])


def gather_shards(near, far):
    return jnp.concatenate([near, from_partner(near, 1), far, from_partner(far, 1)], axis=1)


def half_grads(operands, grads, first):
    width = operands.shape[2] // 4
    return [
        jnp.einsum(
            "erf,erd->efd",
            operands[:, :, k * width : (k + 1) * width],
            grads,
            preferred_element_type=jnp.float32,
        ).astype(jnp.bfloat16)
        for k in (first, first + 1)
    ]


def sum_shards(near, far):
    wide = jnp.float32
    passed = (far[0].astype(wide) + from_partner(far[1], 1).astype(wide)).astype(jnp.bfloat16)
    return (
        near[0].astype(wide)
        + from_partner(near[1], 1).astype(wide)
        + from_partner(passed, 2).astype(wide)
    )


def to_owners(outgoing, local_experts):
    experts_rows, model_width = outgoing.shape
    owners = lax.axis_size("expert")
    capacity = experts_rows // (owners * local_experts)
    received = lax.all_to_all(
        outgoing.reshape(owners, local_experts, capacity, model_width),
        "expert",
        split_axis=0,
        concat_axis=0,
        tiled=True,
    )
    return received.transpose(1, 0, 2, 3).reshape(local_experts, owners * capacity, model_width)


def to_tokens(produced):
    local_experts, rows, model_width = produced.shape
    owners = lax.axis_size("expert")
    capacity = rows // owners
    returned = lax.all_to_all(
        produced.reshape(local_experts, owners, capacity, model_width).transpose(1, 0, 2, 3),
        "expert",
        split_axis=0,
        concat_axis=0,
        tiled=True,
    )
    return returned.reshape(owners * local_experts * capacity, model_width)


def expert_forward(grouped, w_in_use, w_out_use):
    before = jnp.einsum("erd,efd->erf", grouped, w_in_use, preferred_element_type=jnp.float32)
    activated = jax.nn.gelu(before).astype(jnp.bfloat16)
    produced = jnp.einsum("erf,efd->erd", activated, w_out_use, preferred_element_type=jnp.float32)
    return (produced.astype(jnp.bfloat16), (grouped, before, activated))


def expert_backward(grad_rows, before, w_in_use, w_out_use):
    grad_activated = jnp.einsum(
        "erd,efd->erf", grad_rows, w_out_use, preferred_element_type=jnp.float32
    )
    grad_before = jax.vjp(jax.nn.gelu, before)[1](grad_activated)[0].astype(jnp.bfloat16)
    grad_inputs = jnp.einsum(
        "erf,efd->erd", grad_before, w_in_use, preferred_element_type=jnp.float32
    )
    return (grad_inputs.astype(jnp.bfloat16), grad_before)


def dispatch_of(targets, experts):
    length = targets.shape[0]
    capacity = max(2, 2 * length // experts)
    chosen = targets[:, None] == jnp.arange(experts, dtype=jnp.int32)[None, :]
    positions = jnp.arange(length, dtype=jnp.int32)
    earlier = (positions[:, None] > positions[None, :]).astype(jnp.bfloat16)
    counts = jnp.dot(earlier, chosen.astype(jnp.bfloat16), preferred_element_type=jnp.float32)
    slot_rank = jnp.sum(jnp.where(chosen, counts, 0.0), axis=-1).astype(jnp.int32)
    slot_index = targets * capacity + slot_rank
    slots = jnp.arange(experts * capacity, dtype=jnp.int32)
    placement = (slots[:, None] == slot_index[None, :]).astype(jnp.bfloat16)
    return (chosen, placement)


def place(placement, rows):
    return jnp.dot(placement, rows, preferred_element_type=jnp.float32).astype(jnp.bfloat16)


def fetch(placement, rows):
    return jnp.einsum("bs,bd->sd", placement, rows, preferred_element_type=jnp.float32)


def layer_forward(arriving, dispatch, mixer_set, position_bias, w_in_use, w_out_use):
    gain_first, gain_second, w_project, w_output, w_router = mixer_set
    hidden = arriving.astype(jnp.float32)
    length, model_width = hidden.shape
    head_count = position_bias.shape[0]
    head_size = model_width // head_count
    head_shape = (length, head_count, head_size)
    factor = head_size ** (-0.5)
    first_scale = root_scale(hidden)
    normed = (hidden * first_scale * gain_first.astype(jnp.float32)).astype(jnp.bfloat16)
    projected = jnp.dot(normed, w_project, preferred_element_type=jnp.float32).astype(jnp.bfloat16)
    queries, key_rows, value_rows = jnp.split(projected, 3, axis=1)
    scores = (
        jnp.einsum(
            "qhd,khd->hqk",
            queries.reshape(head_shape),
            key_rows.reshape(head_shape),
            preferred_element_type=jnp.float32,
        )
        * factor
        + position_bias
    )
    row_peak = jnp.max(scores, axis=-1, keepdims=True)
    log_total = row_peak + jnp.log(jnp.sum(jnp.exp(scores - row_peak), axis=-1, keepdims=True))
    shares = jnp.exp(scores - log_total).astype(jnp.bfloat16)
    attended = jnp.einsum(
        "hqk,khd->qhd", shares, value_rows.reshape(head_shape), preferred_element_type=jnp.float32
    )
    attended = attended.reshape(length, model_width).astype(jnp.bfloat16)
    mixed = hidden + jnp.dot(attended, w_output, preferred_element_type=jnp.float32)
    second_scale = root_scale(mixed)
    routed = (mixed * second_scale * gain_second.astype(jnp.float32)).astype(jnp.bfloat16)
    logits = jnp.dot(routed, w_router, preferred_element_type=jnp.float32)
    router = jax.nn.softmax(logits, axis=-1)
    chosen, placement = dispatch
    gate_value = jnp.sum(jnp.where(chosen, router, 0.0), axis=-1)
    grouped = to_owners(place(placement, routed), w_in_use.shape[0])
    produced, kept_rows = expert_forward(grouped, w_in_use, w_out_use)
    fetched = fetch(placement, to_tokens(produced))
    result = mixed + gate_value[:, None] * fetched
    stored = (
        hidden,
        normed,
        first_scale,
        queries,
        key_rows,
        value_rows,
        log_total,
        attended,
        mixed,
        second_scale,
        routed,
        router,
        chosen,
        gate_value,
        placement,
        fetched,
        kept_rows,
    )
    return (result, stored)


def layer_backward(grad_out, stored, mixer_set, position_bias, w_in_use, w_out_use, at_experts):
    gain_first, gain_second, w_project, w_output, w_router = mixer_set
    (
        hidden,
        normed,
        first_scale,
        queries,
        key_rows,
        value_rows,
        log_total,
        attended,
        mixed,
        second_scale,
        routed,
        router,
        chosen,
        gate_value,
        placement,
        fetched,
        kept_rows,
    ) = stored
    length, model_width = hidden.shape
    head_count = position_bias.shape[0]
    head_size = model_width // head_count
    head_shape = (length, head_count, head_size)
    factor = head_size ** (-0.5)
    grad_gate = jnp.sum(grad_out * fetched, axis=-1)
    grad_fetched = (gate_value[:, None] * grad_out).astype(jnp.bfloat16)
    grouped, before, activated = kept_rows
    grad_rows = to_owners(place(placement, grad_fetched), w_in_use.shape[0])
    grad_inputs, grad_before = expert_backward(grad_rows, before, w_in_use, w_out_use)
    kept_expert = dict(
        grouped=grouped, activated=activated, grad_rows=grad_rows, grad_before=grad_before
    )
    grad_returned = at_experts(kept_expert, to_tokens(grad_inputs))
    grad_routed = fetch(placement, grad_returned)
    grad_logits = (
        (gate_value * grad_gate)[:, None] * (chosen.astype(jnp.float32) - router)
    ).astype(jnp.bfloat16)
    grad_routed = grad_routed + jnp.einsum(
        "se,de->sd", grad_logits, w_router, preferred_element_type=jnp.float32
    )
    norm_grad, grad_gain_second = norm_backward(
        grad_routed, mixed, second_scale, gain_second.astype(jnp.float32)
    )
    grad_mixed = grad_out + norm_grad
    grad_branch = grad_mixed.astype(jnp.bfloat16)
    grad_attended = jnp.einsum(
        "se,de->sd", grad_branch, w_output, preferred_element_type=jnp.float32
    )
    grad_attended = grad_attended.astype(jnp.bfloat16).reshape(head_shape)
    query_heads = queries.reshape(head_shape)
    key_heads = key_rows.reshape(head_shape)
    scores = (
        jnp.einsum("qhd,khd->hqk", query_heads, key_heads, preferred_element_type=jnp.float32)
        * factor
        + position_bias
    )
    softmax_rows = jnp.exp(scores - log_total)
    shares = softmax_rows.astype(jnp.bfloat16)
    grad_values = jnp.einsum(
        "hqk,qhd->khd", shares, grad_attended, preferred_element_type=jnp.float32
    )
    grad_values = grad_values.astype(jnp.bfloat16).reshape(length, model_width)
    grad_shares = jnp.einsum(
        "qhd,khd->hqk",
        grad_attended,
        value_rows.reshape(head_shape),
        preferred_element_type=jnp.float32,
    )
    grad_scores = softmax_rows * (
        grad_shares - jnp.sum(grad_shares * softmax_rows, axis=-1, keepdims=True)
    )
    grad_scores = grad_scores.astype(jnp.bfloat16)
    grad_queries = (
        jnp.einsum("hqk,khd->qhd", grad_scores, key_heads, preferred_element_type=jnp.float32)
        * factor
    )
    grad_queries = grad_queries.astype(jnp.bfloat16).reshape(length, model_width)
    grad_keys = (
        jnp.einsum("hqk,qhd->khd", grad_scores, query_heads, preferred_element_type=jnp.float32)
        * factor
    )
    grad_keys = grad_keys.astype(jnp.bfloat16).reshape(length, model_width)
    grad_projected = jnp.concatenate([grad_queries, grad_keys, grad_values], axis=1)
    grad_normed = jnp.einsum(
        "se,de->sd", grad_projected, w_project, preferred_element_type=jnp.float32
    )
    first_grad, grad_gain_first = norm_backward(
        grad_normed, hidden, first_scale, gain_first.astype(jnp.float32)
    )
    grad_hidden = grad_mixed + first_grad
    kept = dict(
        gains=jnp.stack([grad_gain_first, grad_gain_second], axis=1),
        grad_scores=grad_scores,
        normed=normed,
        grad_projected=grad_projected,
        attended=attended,
        grad_branch=grad_branch,
        routed=routed,
        grad_logits=grad_logits,
    )
    return (grad_hidden, kept)


def scatter_sum(full, axis):
    return lax.psum_scatter(full, "dp", scatter_dimension=axis, tiled=True)


def weight_grad(operands, grads):
    return jnp.einsum("sd,se->de", operands, grads, preferred_element_type=jnp.float32)


def reduce_mixer(rows, sums, buckets):
    project = weight_grad(rows["normed"], rows["grad_projected"])
    output = weight_grad(rows["attended"], rows["grad_branch"])
    router = weight_grad(rows["routed"], rows["grad_logits"])
    table = bucket_sums(sums["grad_scores"], buckets)
    small = pack_small([router, sums["gains"]], table)
    packed = jnp.concatenate([project, output, small], axis=1).astype(jnp.bfloat16)
    total = lax.psum(scatter_sum(packed, 0), "expert").astype(jnp.float32)
    width = total.shape[0] * lax.axis_size("dp")
    query, key, value, output = (total[:, i * width : (i + 1) * width] for i in range(4))
    router, gains, table = unpack_small(
        total[:, 4 * width :], [router.shape[1], 2], table.shape, 1
    )
    return (gains[:, 0], gains[:, 1], query, key, value, output, router, table)


def pack_small(columns, table, shards=None):
    rows = columns[0].shape[0]
    shards = lax.axis_size("dp") if shards is None else shards
    own = table.reshape(shards, table.shape[0] // shards, table.shape[1])
    own = jnp.pad(own, ((0, 0), (0, rows // shards - own.shape[1]), (0, 0)))
    packed = jnp.concatenate([*columns, own.reshape(rows, table.shape[1])], axis=1)
    return jnp.pad(packed, ((0, 0), (0, -packed.shape[1] % 128)))


def unpack_small(packed, widths, table_shape, shards):
    found = []
    start = 0
    for width in widths:
        found.append(packed[:, start : start + width])
        start += width
    table_rows, heads = table_shape
    table_rows = table_rows * shards // lax.axis_size("dp")
    table = packed[:, start : start + heads].reshape(shards, -1, heads)
    found.append(table[:, : table_rows // shards].reshape(table_rows, heads))
    return found


def local(
    ends,
    routes,
    norm_gain_first,
    norm_gain_second,
    w_query,
    w_key,
    w_value,
    w_output,
    w_router,
    bias_table,
    expert_in,
    expert_out,
):
    is_first = lax.axis_index("section") == 0
    model_width = ends.shape[2]
    shards = lax.axis_size("dp")
    experts = w_router.shape[2]
    gains = jnp.stack([norm_gain_first[0], norm_gain_second[0]], axis=1)
    small = pack_small([w_router[0], gains], bias_table[0], 1)
    packed = jnp.concatenate([w_query[0], w_key[0], w_value[0], w_output[0], small], axis=1)
    packed = lax.all_gather(packed, "dp", axis=0, tiled=True)
    far_in = from_partner(expert_in[0], 2)
    far_in, near_out = lax.optimization_barrier((far_in, expert_out[0]))
    far_out = from_partner(near_out, 2)
    w_in_use = gather_shards(expert_in[0], far_in)
    w_out_use = gather_shards(expert_out[0], far_out)
    buckets = bias_table.shape[1] * shards
    router_full, gains, bias_rows = unpack_small(
        packed[:, 4 * model_width :],
        [experts, 2],
        (buckets * shards // shards, bias_table.shape[2]),
        shards,
    )
    mixer_set = (
        gains[:, 0],
        gains[:, 1],
        packed[:, : 3 * model_width],
        packed[:, 3 * model_width : 4 * model_width],
        router_full,
    )
    position_bias = bias_of(bias_rows.astype(jnp.float32), SEQ)
    local_rows = ends[0]
    local_routes = routes[0, :, 0]

    def block_rows(source, micro_index):
        return source[micro_index * SEQ : (micro_index + 1) * SEQ]

    dispatches = [dispatch_of(block_rows(local_routes, m), experts) for m in range(MICRO)]
    stored_list = []
    results = []
    arriving = jnp.zeros((SEQ, model_width), jnp.bfloat16)
    for tick_number in range(MICRO + 1):
        own_micro = min(tick_number, MICRO - 1)
        prior_micro = max(tick_number - 1, 0)
        layer_input = jnp.where(is_first, block_rows(local_rows, own_micro), arriving)
        dispatch = jax.tree.map(
            lambda own, prior: jnp.where(is_first, own, prior),
            dispatches[own_micro],
            dispatches[prior_micro],
        )
        result, stored = layer_forward(
            layer_input, dispatch, mixer_set, position_bias, w_in_use, w_out_use
        )
        stored_list.append(stored)
        results.append(result)
        if tick_number < MICRO:
            arriving = from_behind(result.astype(jnp.bfloat16), "section", 1)
    input_grads = [None] * MICRO
    returning = jnp.zeros((SEQ, model_width), jnp.bfloat16)
    mixer_kept = []
    expert_kept = []
    expert_sum = []

    def real(kept, name):
        return (kept[1][name], jnp.where(is_first, kept[2][name], kept[0][name]))

    def at_experts(kept, returned):
        expert_kept.append(kept)
        if len(expert_kept) <= MICRO:
            return returned
        rows = {name: jnp.concatenate(real(expert_kept, name), axis=1) for name in kept}
        halves = [
            half_grads(rows[operand], rows[grads], first)
            for operand, grads in (("activated", "grad_rows"), ("grad_before", "grouped"))
            for first in (2, 0)
        ]
        returned, halves = lax.optimization_barrier((returned, halves))
        far_out, near_out, far_in, near_in = halves
        expert_sum.extend([sum_shards(near_in, far_in), sum_shards(near_out, far_out)])
        return returned

    for step_number in range(MICRO + 1):
        if step_number < MICRO:
            cotangent = block_rows(local_rows, MICRO - 1 - step_number).astype(jnp.float32)
        else:
            cotangent = jnp.zeros((SEQ, model_width), jnp.float32)
        grad_out = jnp.where(is_first, returning.astype(jnp.float32), cotangent)
        grad_hidden, kept_mixer = layer_backward(
            grad_out,
            stored_list[MICRO - step_number],
            mixer_set,
            position_bias,
            w_in_use,
            w_out_use,
            at_experts,
        )
        if step_number < MICRO:
            returning = from_behind(grad_hidden.astype(jnp.bfloat16), "section", -1)
        if step_number >= 1:
            input_grads[MICRO - step_number] = grad_hidden
        mixer_kept.append(kept_mixer)

    summed = ("gains", "grad_scores")
    sums = {
        name: sum(part.astype(jnp.float32) for part in real(mixer_kept, name)) for name in summed
    }
    rows = {
        name: jnp.concatenate(real(mixer_kept, name), axis=0)
        for name in mixer_kept[0]
        if name not in summed
    }
    mixer_sum = reduce_mixer(rows, sums, buckets)
    pieces = [
        jnp.where(is_first, input_grads[micro_index], results[micro_index + 1])
        for micro_index in range(MICRO)
    ]
    boundary = jnp.concatenate(pieces, axis=0)[None]
    return (
        boundary,
        mixer_sum[0][None],
        mixer_sum[1][None],
        mixer_sum[2][None],
        mixer_sum[3][None],
        mixer_sum[4][None],
        mixer_sum[5][None],
        mixer_sum[6][None],
        mixer_sum[7][None],
        expert_sum[0][None],
        expert_sum[1][None],
    )


def solution(mesh):
    in_specs = (
        P("section", ("expert", "dp"), None),
        P("section", ("expert", "dp"), None),
        P("section", "dp"),
        P("section", "dp"),
        P("section", "dp", None),
        P("section", "dp", None),
        P("section", "dp", None),
        P("section", "dp", None),
        P("section", "dp", None),
        P("section", "dp", None),
        P("section", "expert", "dp", None),
        P("section", "expert", "dp", None),
    )
    out_specs = (
        P("section", ("expert", "dp"), None),
        P("section", "dp"),
        P("section", "dp"),
        P("section", "dp", None),
        P("section", "dp", None),
        P("section", "dp", None),
        P("section", "dp", None),
        P("section", "dp", None),
        P("section", "dp", None),
        P("section", "expert", "dp", None),
        P("section", "expert", "dp", None),
    )
    return jax.shard_map(local, mesh=mesh, in_specs=in_specs, out_specs=out_specs, check_vma=False)
```

```python
import jax
import jax.numpy as jnp
import numpy as np
from jax import lax
from jax.experimental import pallas as pl
from jax.experimental.pallas import tpu as pltpu
from jax.sharding import PartitionSpec as P

SEQ = 256
MICRO = 2


EPSILON = 1e-06
LIMITS = (1, 2, 3, 4, 5, 6, 7, 8, 12, 16, 23, 32, 46, 64, 91)


def from_behind(block, axis, distance):
    devices = range(lax.axis_size(axis))
    route = [(i - distance, i) for i in devices if i - distance in devices]
    return lax.ppermute(block, axis, route)


def bucket_grid(length, buckets):
    positions = jnp.arange(length, dtype=jnp.int32)
    offsets = positions[:, None] - positions[None, :]
    distance = jnp.abs(offsets)
    bucket = jnp.where(offsets < 0, buckets // 2, 0).astype(jnp.int32)
    for threshold in LIMITS:
        bucket = bucket + (distance >= threshold).astype(jnp.int32)
    return bucket


def known_buckets(length, buckets):
    positions = np.arange(length)
    offsets = positions[:, None] - positions[None, :]
    known = np.where(offsets < 0, buckets // 2, 0)
    for threshold in LIMITS:
        known = known + (np.abs(offsets) >= threshold)
    return known


def bias_of(bias_rows, length):
    buckets, head_count = bias_rows.shape
    high, wide = 8, 128
    known = known_buckets(length, buckets)

    def kernel(grid_ref, table_ref, bias_ref):
        start = pl.program_id(0) * buckets
        values = [table_ref[start + number] for number in range(buckets)]
        for top in range(0, length, high):
            for left in range(0, length, wide):
                block = (slice(top, top + high), slice(left, left + wide))
                first, *others = np.unique(known[block]).tolist()
                bias = jnp.full((high, wide), values[first], jnp.float32)
                if others:
                    named = grid_ref[block]
                    for number in others:
                        bias = jnp.where(named == number, values[number], bias)
                bias_ref[(0,) + block] = bias

    return pl.pallas_call(
        kernel,
        grid=(head_count,),
        out_shape=jax.ShapeDtypeStruct((head_count, length, length), jnp.float32),
        in_specs=[
            pl.BlockSpec((length, length), lambda h: (0, 0)),
            pl.BlockSpec(memory_space=pltpu.SMEM),
        ],
        out_specs=pl.BlockSpec((1, length, length), lambda h: (h, 0, 0)),
        compiler_params=pltpu.CompilerParams(vmem_limit_bytes=16 * 1024 * 1024),
        cost_estimate=pl.CostEstimate(
            flops=20 * head_count * length * length,
            bytes_accessed=4 * head_count * length * length,
            transcendentals=0,
        ),
    )(bucket_grid(length, buckets), bias_rows.T.reshape(-1))


def bucket_sums(grid_grads, buckets):
    head_count, length, _ = grid_grads.shape
    high, wide = 8, 128
    known = known_buckets(length, buckets)

    def kernel(grid_ref, grads_ref, table_ref):
        sums = [None] * buckets
        for top in range(0, length, high):
            for left in range(0, length, wide):
                block = (slice(top, top + high), slice(left, left + wide))
                present = np.unique(known[block])
                grads = grads_ref[(0,) + block]
                named = grid_ref[block] if len(present) > 1 else None
                for number in present.tolist():
                    own = grads if named is None else jnp.where(named == number, grads, 0.0)
                    sums[number] = own if sums[number] is None else sums[number] + own
        empty = jnp.zeros((1, wide), jnp.float32)
        table_ref[0] = jnp.concatenate(
            [empty if own is None else jnp.sum(own, axis=0, keepdims=True) for own in sums], axis=0
        )

    partial = pl.pallas_call(
        kernel,
        grid=(head_count,),
        out_shape=jax.ShapeDtypeStruct((head_count, buckets, wide), jnp.float32),
        in_specs=[
            pl.BlockSpec((length, length), lambda h: (0, 0)),
            pl.BlockSpec((1, length, length), lambda h: (h, 0, 0)),
        ],
        out_specs=pl.BlockSpec((1, buckets, wide), lambda h: (h, 0, 0)),
        compiler_params=pltpu.CompilerParams(vmem_limit_bytes=16 * 1024 * 1024),
        cost_estimate=pl.CostEstimate(
            flops=30 * grid_grads.size, bytes_accessed=5 * grid_grads.size, transcendentals=0
        ),
    )(bucket_grid(length, buckets), grid_grads)
    return jnp.sum(partial, axis=-1).T


def root_scale(values):
    return lax.rsqrt(jnp.mean(values * values, axis=-1, keepdims=True) + EPSILON)


def norm_backward(grad_normed, values, factor, gain_value):
    scaled = grad_normed * gain_value
    grad_gain = jnp.sum(grad_normed * values * factor, axis=0)
    grad_values = factor * scaled - values * factor * factor * factor * jnp.mean(
        scaled * values, axis=-1, keepdims=True
    )
    return (grad_values, grad_gain)


def from_partner(block, bit):
    return lax.ppermute(block, "dp", [(i, i ^ bit) for i in range(lax.axis_size("dp"))])


def gather_shards(near, far):
    return jnp.concatenate([near, from_partner(near, 1), far, from_partner(far, 1)], axis=1)


def half_grads(operands, grads, first):
    width = operands.shape[2] // 4
    return [
        jnp.einsum(
            "erf,erd->efd",
            operands[:, :, k * width : (k + 1) * width],
            grads,
            preferred_element_type=jnp.float32,
        ).astype(jnp.bfloat16)
        for k in (first, first + 1)
    ]


def pass_on(near, far):
    wide = jnp.float32
    passed = (far[0].astype(wide) + from_partner(far[1], 1).astype(wide)).astype(jnp.bfloat16)
    return (near[0], from_partner(near[1], 1), passed)


def add_shards(own, crossed, arrived):
    wide = jnp.float32
    return own.astype(wide) + crossed.astype(wide) + arrived.astype(wide)


def to_owners(outgoing, local_experts):
    experts_rows, model_width = outgoing.shape
    owners = lax.axis_size("expert")
    capacity = experts_rows // (owners * local_experts)
    received = lax.all_to_all(
        outgoing.reshape(owners, local_experts, capacity, model_width),
        "expert",
        split_axis=0,
        concat_axis=0,
        tiled=True,
    )
    return received.transpose(1, 0, 2, 3).reshape(local_experts, owners * capacity, model_width)


def to_tokens(produced):
    local_experts, rows, model_width = produced.shape
    owners = lax.axis_size("expert")
    capacity = rows // owners
    returned = lax.all_to_all(
        produced.reshape(local_experts, owners, capacity, model_width).transpose(1, 0, 2, 3),
        "expert",
        split_axis=0,
        concat_axis=0,
        tiled=True,
    )
    return returned.reshape(owners * local_experts * capacity, model_width)


def expert_forward(grouped, w_in_use, w_out_use):
    before = jnp.einsum("erd,efd->erf", grouped, w_in_use, preferred_element_type=jnp.float32)
    activated = jax.nn.gelu(before).astype(jnp.bfloat16)
    produced = jnp.einsum("erf,efd->erd", activated, w_out_use, preferred_element_type=jnp.float32)
    return (produced.astype(jnp.bfloat16), (grouped, before, activated))


def expert_backward(grad_rows, before, w_in_use, w_out_use):
    grad_activated = jnp.einsum(
        "erd,efd->erf", grad_rows, w_out_use, preferred_element_type=jnp.float32
    )
    grad_before = jax.vjp(jax.nn.gelu, before)[1](grad_activated)[0].astype(jnp.bfloat16)
    grad_inputs = jnp.einsum(
        "erf,efd->erd", grad_before, w_in_use, preferred_element_type=jnp.float32
    )
    return (grad_inputs.astype(jnp.bfloat16), grad_before)


def dispatch_of(targets, experts):
    length = targets.shape[0]
    capacity = max(2, 2 * length // experts)
    chosen = targets[:, None] == jnp.arange(experts, dtype=jnp.int32)[None, :]
    positions = jnp.arange(length, dtype=jnp.int32)
    earlier = (positions[:, None] > positions[None, :]).astype(jnp.bfloat16)
    counts = jnp.dot(earlier, chosen.astype(jnp.bfloat16), preferred_element_type=jnp.float32)
    slot_rank = jnp.sum(jnp.where(chosen, counts, 0.0), axis=-1).astype(jnp.int32)
    slot_index = targets * capacity + slot_rank
    slots = jnp.arange(experts * capacity, dtype=jnp.int32)
    placement = (slots[:, None] == slot_index[None, :]).astype(jnp.bfloat16)
    return (chosen, placement)


def place(placement, rows):
    return jnp.dot(placement, rows, preferred_element_type=jnp.float32).astype(jnp.bfloat16)


def fetch(placement, rows):
    return jnp.einsum("bs,bd->sd", placement, rows, preferred_element_type=jnp.float32)


def layer_forward(arriving, dispatch, mixer_set, position_bias, w_in_use, w_out_use):
    gain_first, gain_second, w_project, w_output, w_router = mixer_set
    hidden = arriving.astype(jnp.float32)
    length, model_width = hidden.shape
    head_count = position_bias.shape[0]
    head_size = model_width // head_count
    head_shape = (length, head_count, head_size)
    factor = head_size ** (-0.5)
    first_scale = root_scale(hidden)
    normed = (hidden * first_scale * gain_first.astype(jnp.float32)).astype(jnp.bfloat16)
    projected = jnp.dot(normed, w_project, preferred_element_type=jnp.float32).astype(jnp.bfloat16)
    queries, key_rows, value_rows = jnp.split(projected, 3, axis=1)
    scores = (
        jnp.einsum(
            "qhd,khd->hqk",
            queries.reshape(head_shape),
            key_rows.reshape(head_shape),
            preferred_element_type=jnp.float32,
        )
        * factor
        + position_bias
    )
    row_peak = jnp.max(scores, axis=-1, keepdims=True)
    log_total = row_peak + jnp.log(jnp.sum(jnp.exp(scores - row_peak), axis=-1, keepdims=True))
    shares = jnp.exp(scores - log_total).astype(jnp.bfloat16)
    attended = jnp.einsum(
        "hqk,khd->qhd", shares, value_rows.reshape(head_shape), preferred_element_type=jnp.float32
    )
    attended = attended.reshape(length, model_width).astype(jnp.bfloat16)
    mixed = hidden + jnp.dot(attended, w_output, preferred_element_type=jnp.float32)
    second_scale = root_scale(mixed)
    routed = (mixed * second_scale * gain_second.astype(jnp.float32)).astype(jnp.bfloat16)
    logits = jnp.dot(routed, w_router, preferred_element_type=jnp.float32)
    router = jax.nn.softmax(logits, axis=-1)
    chosen, placement = dispatch
    gate_value = jnp.sum(jnp.where(chosen, router, 0.0), axis=-1)
    grouped = to_owners(place(placement, routed), w_in_use.shape[0])
    produced, kept_rows = expert_forward(grouped, w_in_use, w_out_use)
    fetched = fetch(placement, to_tokens(produced))
    result = mixed + gate_value[:, None] * fetched
    stored = (
        hidden,
        normed,
        first_scale,
        queries,
        key_rows,
        value_rows,
        log_total,
        attended,
        mixed,
        second_scale,
        routed,
        router,
        chosen,
        gate_value,
        placement,
        fetched,
        kept_rows,
    )
    return (result, stored)


def layer_backward(grad_out, stored, mixer_set, position_bias, w_in_use, w_out_use, at_experts):
    gain_first, gain_second, w_project, w_output, w_router = mixer_set
    (
        hidden,
        normed,
        first_scale,
        queries,
        key_rows,
        value_rows,
        log_total,
        attended,
        mixed,
        second_scale,
        routed,
        router,
        chosen,
        gate_value,
        placement,
        fetched,
        kept_rows,
    ) = stored
    length, model_width = hidden.shape
    head_count = position_bias.shape[0]
    head_size = model_width // head_count
    head_shape = (length, head_count, head_size)
    factor = head_size ** (-0.5)
    grad_gate = jnp.sum(grad_out * fetched, axis=-1)
    grad_fetched = (gate_value[:, None] * grad_out).astype(jnp.bfloat16)
    grouped, before, activated = kept_rows
    grad_rows = to_owners(place(placement, grad_fetched), w_in_use.shape[0])
    grad_inputs, grad_before = expert_backward(grad_rows, before, w_in_use, w_out_use)
    kept_expert = dict(
        grouped=grouped, activated=activated, grad_rows=grad_rows, grad_before=grad_before
    )
    grad_returned = at_experts(kept_expert, to_tokens(grad_inputs))
    grad_routed = fetch(placement, grad_returned)
    grad_logits = (
        (gate_value * grad_gate)[:, None] * (chosen.astype(jnp.float32) - router)
    ).astype(jnp.bfloat16)
    grad_routed = grad_routed + jnp.einsum(
        "se,de->sd", grad_logits, w_router, preferred_element_type=jnp.float32
    )
    norm_grad, grad_gain_second = norm_backward(
        grad_routed, mixed, second_scale, gain_second.astype(jnp.float32)
    )
    grad_mixed = grad_out + norm_grad
    grad_branch = grad_mixed.astype(jnp.bfloat16)
    grad_attended = jnp.einsum(
        "se,de->sd", grad_branch, w_output, preferred_element_type=jnp.float32
    )
    grad_attended = grad_attended.astype(jnp.bfloat16).reshape(head_shape)
    query_heads = queries.reshape(head_shape)
    key_heads = key_rows.reshape(head_shape)
    scores = (
        jnp.einsum("qhd,khd->hqk", query_heads, key_heads, preferred_element_type=jnp.float32)
        * factor
        + position_bias
    )
    softmax_rows = jnp.exp(scores - log_total)
    shares = softmax_rows.astype(jnp.bfloat16)
    grad_values = jnp.einsum(
        "hqk,qhd->khd", shares, grad_attended, preferred_element_type=jnp.float32
    )
    grad_values = grad_values.astype(jnp.bfloat16).reshape(length, model_width)
    grad_shares = jnp.einsum(
        "qhd,khd->hqk",
        grad_attended,
        value_rows.reshape(head_shape),
        preferred_element_type=jnp.float32,
    )
    grad_scores = softmax_rows * (
        grad_shares - jnp.sum(grad_shares * softmax_rows, axis=-1, keepdims=True)
    )
    grad_scores = grad_scores.astype(jnp.bfloat16)
    grad_queries = (
        jnp.einsum("hqk,khd->qhd", grad_scores, key_heads, preferred_element_type=jnp.float32)
        * factor
    )
    grad_queries = grad_queries.astype(jnp.bfloat16).reshape(length, model_width)
    grad_keys = (
        jnp.einsum("hqk,qhd->khd", grad_scores, query_heads, preferred_element_type=jnp.float32)
        * factor
    )
    grad_keys = grad_keys.astype(jnp.bfloat16).reshape(length, model_width)
    grad_projected = jnp.concatenate([grad_queries, grad_keys, grad_values], axis=1)
    grad_normed = jnp.einsum(
        "se,de->sd", grad_projected, w_project, preferred_element_type=jnp.float32
    )
    first_grad, grad_gain_first = norm_backward(
        grad_normed, hidden, first_scale, gain_first.astype(jnp.float32)
    )
    grad_hidden = grad_mixed + first_grad
    kept = dict(
        gains=jnp.stack([grad_gain_first, grad_gain_second], axis=1),
        grad_scores=grad_scores,
        normed=normed,
        grad_projected=grad_projected,
        attended=attended,
        grad_branch=grad_branch,
        routed=routed,
        grad_logits=grad_logits,
    )
    return (grad_hidden, kept)


def scatter_sum(full, axis):
    return lax.psum_scatter(full, "dp", scatter_dimension=axis, tiled=True)


def weight_grad(operands, grads):
    return jnp.einsum("sd,se->de", operands, grads, preferred_element_type=jnp.float32)


def reduce_mixer(rows, sums, buckets, expert_pairs):
    project = weight_grad(rows["normed"], rows["grad_projected"])
    output = weight_grad(rows["attended"], rows["grad_branch"])
    router = weight_grad(rows["routed"], rows["grad_logits"])
    table = bucket_sums(sums["grad_scores"], buckets)
    small = pack_small([router, sums["gains"]], table)
    packed = jnp.concatenate([project, output, small], axis=1).astype(jnp.bfloat16)
    (own_in, crossed_in, passed_in), (own_out, crossed_out, passed_out) = expert_pairs
    packed, arrived_out = lax.optimization_barrier((packed, from_partner(passed_out, 2)))
    scattered = scatter_sum(packed, 0)
    scattered, passed_in = lax.optimization_barrier((scattered, passed_in))
    arrived_in = from_partner(passed_in, 2)
    total = lax.psum(scattered, "expert").astype(jnp.float32)
    expert_sum = (
        add_shards(own_in, crossed_in, arrived_in),
        add_shards(own_out, crossed_out, arrived_out),
    )
    width = total.shape[0] * lax.axis_size("dp")
    query, key, value, output = (total[:, i * width : (i + 1) * width] for i in range(4))
    router, gains, table = unpack_small(
        total[:, 4 * width :], [router.shape[1], 2], table.shape, 1
    )
    return (gains[:, 0], gains[:, 1], query, key, value, output, router, table), expert_sum


def pack_small(columns, table, shards=None):
    rows = columns[0].shape[0]
    shards = lax.axis_size("dp") if shards is None else shards
    own = table.reshape(shards, table.shape[0] // shards, table.shape[1])
    own = jnp.pad(own, ((0, 0), (0, rows // shards - own.shape[1]), (0, 0)))
    packed = jnp.concatenate([*columns, own.reshape(rows, table.shape[1])], axis=1)
    return jnp.pad(packed, ((0, 0), (0, -packed.shape[1] % 128)))


def unpack_small(packed, widths, table_shape, shards):
    found = []
    start = 0
    for width in widths:
        found.append(packed[:, start : start + width])
        start += width
    table_rows, heads = table_shape
    table_rows = table_rows * shards // lax.axis_size("dp")
    table = packed[:, start : start + heads].reshape(shards, -1, heads)
    found.append(table[:, : table_rows // shards].reshape(table_rows, heads))
    return found


def local(
    ends,
    routes,
    norm_gain_first,
    norm_gain_second,
    w_query,
    w_key,
    w_value,
    w_output,
    w_router,
    bias_table,
    expert_in,
    expert_out,
):
    is_first = lax.axis_index("section") == 0
    model_width = ends.shape[2]
    shards = lax.axis_size("dp")
    experts = w_router.shape[2]
    gains = jnp.stack([norm_gain_first[0], norm_gain_second[0]], axis=1)
    small = pack_small([w_router[0], gains], bias_table[0], 1)
    packed = jnp.concatenate([w_query[0], w_key[0], w_value[0], w_output[0], small], axis=1)
    packed = lax.all_gather(packed, "dp", axis=0, tiled=True)
    far_in = from_partner(expert_in[0], 2)
    packed, near_out = lax.optimization_barrier((packed, expert_out[0]))
    far_out = from_partner(near_out, 2)
    w_in_use = gather_shards(expert_in[0], far_in)
    w_out_use = gather_shards(expert_out[0], far_out)
    buckets = bias_table.shape[1] * shards
    router_full, gains, bias_rows = unpack_small(
        packed[:, 4 * model_width :],
        [experts, 2],
        (buckets * shards // shards, bias_table.shape[2]),
        shards,
    )
    mixer_set = (
        gains[:, 0],
        gains[:, 1],
        packed[:, : 3 * model_width],
        packed[:, 3 * model_width : 4 * model_width],
        router_full,
    )
    position_bias = bias_of(bias_rows.astype(jnp.float32), SEQ)
    local_rows = ends[0]
    local_routes = routes[0, :, 0]

    def block_rows(source, micro_index):
        return source[micro_index * SEQ : (micro_index + 1) * SEQ]

    dispatches = [dispatch_of(block_rows(local_routes, m), experts) for m in range(MICRO)]
    stored_list = []
    results = []
    arriving = jnp.zeros((SEQ, model_width), jnp.bfloat16)
    for tick_number in range(MICRO + 1):
        own_micro = min(tick_number, MICRO - 1)
        prior_micro = max(tick_number - 1, 0)
        layer_input = jnp.where(is_first, block_rows(local_rows, own_micro), arriving)
        dispatch = jax.tree.map(
            lambda own, prior: jnp.where(is_first, own, prior),
            dispatches[own_micro],
            dispatches[prior_micro],
        )
        result, stored = layer_forward(
            layer_input, dispatch, mixer_set, position_bias, w_in_use, w_out_use
        )
        stored_list.append(stored)
        results.append(result)
        if tick_number < MICRO:
            arriving = from_behind(result.astype(jnp.bfloat16), "section", 1)
    input_grads = [None] * MICRO
    returning = jnp.zeros((SEQ, model_width), jnp.bfloat16)
    mixer_kept = []
    expert_kept = []
    expert_sum = []

    def real(kept, name):
        return (kept[1][name], jnp.where(is_first, kept[2][name], kept[0][name]))

    def at_experts(kept, returned):
        expert_kept.append(kept)
        if len(expert_kept) <= MICRO:
            return returned
        rows = {name: jnp.concatenate(real(expert_kept, name), axis=1) for name in kept}
        halves = [
            half_grads(rows[operand], rows[grads], first)
            for operand, grads in (("activated", "grad_rows"), ("grad_before", "grouped"))
            for first in (2, 0)
        ]
        far_out, near_out, far_in, near_in = halves
        pairs = (pass_on(near_in, far_in), pass_on(near_out, far_out))
        returned, pairs = lax.optimization_barrier((returned, pairs))
        expert_sum.extend(pairs)
        return returned

    for step_number in range(MICRO + 1):
        if step_number < MICRO:
            cotangent = block_rows(local_rows, MICRO - 1 - step_number).astype(jnp.float32)
        else:
            cotangent = jnp.zeros((SEQ, model_width), jnp.float32)
        grad_out = jnp.where(is_first, returning.astype(jnp.float32), cotangent)
        grad_hidden, kept_mixer = layer_backward(
            grad_out,
            stored_list[MICRO - step_number],
            mixer_set,
            position_bias,
            w_in_use,
            w_out_use,
            at_experts,
        )
        if step_number < MICRO:
            returning = from_behind(grad_hidden.astype(jnp.bfloat16), "section", -1)
        if step_number >= 1:
            input_grads[MICRO - step_number] = grad_hidden
        mixer_kept.append(kept_mixer)

    summed = ("gains", "grad_scores")
    sums = {
        name: sum(part.astype(jnp.float32) for part in real(mixer_kept, name)) for name in summed
    }
    rows = {
        name: jnp.concatenate(real(mixer_kept, name), axis=0)
        for name in mixer_kept[0]
        if name not in summed
    }
    mixer_sum, expert_sum = reduce_mixer(rows, sums, buckets, expert_sum)
    pieces = [
        jnp.where(is_first, input_grads[micro_index], results[micro_index + 1])
        for micro_index in range(MICRO)
    ]
    boundary = jnp.concatenate(pieces, axis=0)[None]
    return (
        boundary,
        mixer_sum[0][None],
        mixer_sum[1][None],
        mixer_sum[2][None],
        mixer_sum[3][None],
        mixer_sum[4][None],
        mixer_sum[5][None],
        mixer_sum[6][None],
        mixer_sum[7][None],
        expert_sum[0][None],
        expert_sum[1][None],
    )


def solution(mesh):
    in_specs = (
        P("section", ("expert", "dp"), None),
        P("section", ("expert", "dp"), None),
        P("section", "dp"),
        P("section", "dp"),
        P("section", "dp", None),
        P("section", "dp", None),
        P("section", "dp", None),
        P("section", "dp", None),
        P("section", "dp", None),
        P("section", "dp", None),
        P("section", "expert", "dp", None),
        P("section", "expert", "dp", None),
    )
    out_specs = (
        P("section", ("expert", "dp"), None),
        P("section", "dp"),
        P("section", "dp"),
        P("section", "dp", None),
        P("section", "dp", None),
        P("section", "dp", None),
        P("section", "dp", None),
        P("section", "dp", None),
        P("section", "dp", None),
        P("section", "expert", "dp", None),
        P("section", "expert", "dp", None),
    )
    return jax.shard_map(local, mesh=mesh, in_specs=in_specs, out_specs=out_specs, check_vma=False)
```
